32 devices in a mesh: grp: 2 (over y), seq: 16 (over z, x, core).
Axes of the slice: x: 2, y: 2, z: 4, core: 2. Of those that a mesh axis runs over, the one named last changes fastest.
Arguments:
- query_rows: bfloat16 [6144, 4096], P(('grp', 'seq')), parts along dimension 0, may hold values from -0.59765625 to 0.59765625
- key_rows: bfloat16 [6144, 4096], P(('grp', 'seq')), parts along dimension 0, may hold values from -0.59765625 to 0.59765625
- value_rows: bfloat16 [6144, 4096], P(('grp', 'seq')), parts along dimension 0, may hold values from -0.59765625 to 0.59765625
- log_decay: float32 [32, 6144], P(None, ('grp', 'seq')), parts along dimension 1, may hold values from -1 to 0, as said below
- out_grad: bfloat16 [6144, 4096], P(('grp', 'seq')), parts along dimension 0, may hold values from -0.59765625 to 0.59765625
Outputs:
- attended: bfloat16 [6144, 4096], P(('grp', 'seq')), parts along dimension 0
- query_grad: bfloat16 [6144, 4096], P(('grp', 'seq')), parts along dimension 0
- key_grad: bfloat16 [6144, 4096], P(('grp', 'seq')), parts along dimension 0
- value_grad: bfloat16 [6144, 4096], P(('grp', 'seq')), parts along dimension 0
The draws below stay inside these ranges and needn't reach their ends.
There are 2 independent parts, one for each index of `grp`. The reference program is written for one: setup_inputs(seed, part) draws one part's arguments, and reference() takes and returns one part's arrays. A program takes and returns all parts, laid end to end along the dimension named above; each array names one. Nothing has to cross between parts.
Inputs may be any that keep to these rules, and one draw needn't show every extreme that they name: `log_decay`: strictly negative.
All inputs are finite; a program needn't handle non-finite values.
Results may differ from the reference program's by a relative error of at most 0.0057.
Values sent between devices are 32-bit elements; how exact they have to be, the bound alone decides.
A program may use at most 128 MiB of HBM per device.

```python
import jax
import jax.numpy as jnp
from jax import lax

DEVICE_HEAD_SLOTS = 32
HD = 128
TOK_DEV = 192
STEP_TOTAL = 3072


def draw_log_decay(key, part):
    key = jax.random.fold_in(key, 11)
    seed_quick_group, seed_forget_speed, seed_gradual_group, seed_jitter, seed_segment, seed_spike_location, seed_spike = jax.random.split(key, 7)
    fast_share = 0.5
    fast_heads = jax.random.bernoulli(seed_quick_group, fast_share, (DEVICE_HEAD_SLOTS, 1))
    fast_rate = jax.random.uniform(seed_forget_speed, (DEVICE_HEAD_SLOTS, 1), jnp.float32, 1.0 / 50.0, 1.0 / 30.0)
    slow_rate = jnp.exp(jax.random.uniform(seed_gradual_group, (DEVICE_HEAD_SLOTS, 1), jnp.float32, jnp.log(0.05), jnp.log(0.3))) / STEP_TOTAL
    default_forget_speed = jnp.where(fast_heads, fast_rate, slow_rate)
    forget_jitter_level = jax.random.uniform(seed_jitter, (DEVICE_HEAD_SLOTS, STEP_TOTAL), jnp.float32, 0.5, 1.5)
    segment_scale_factor = jnp.exp(jax.random.uniform(seed_segment, (1, STEP_TOTAL // TOK_DEV), jnp.float32, jnp.log(0.5), jnp.log(2.0)))
    segment_scale_factor = jnp.repeat(segment_scale_factor, TOK_DEV, axis=1)
    spike_indices = jax.random.randint(seed_spike_location, (3,), 0, STEP_TOTAL)
    spike_magnitude = jax.random.uniform(seed_spike, (DEVICE_HEAD_SLOTS, 3), jnp.float32, jnp.log(0.6), jnp.log(0.8))
    element_offset = lax.broadcasted_iota(jnp.int32, (1, STEP_TOTAL), 1)
    spike_occurrences = jnp.zeros((DEVICE_HEAD_SLOTS, STEP_TOTAL), jnp.float32)
    for spike_number in range(3):
        spike_occurrences = spike_occurrences + jnp.where(element_offset == spike_indices[spike_number], spike_magnitude[:, spike_number:spike_number + 1], 0.0)
    return -default_forget_speed * forget_jitter_level * segment_scale_factor + spike_occurrences


def block_scale(rng, dims, pieces, low, largest):
    factor_of = 1.0
    for position, parts in pieces:
        steps = jax.random.uniform(jax.random.fold_in(jax.random.fold_in(rng, 6), position), (parts,), jnp.float32, low / len(pieces), largest / len(pieces))
        factor_of = factor_of * jnp.repeat(jnp.exp(steps), dims[position] // parts).reshape((-1,) + (1,) * (len(dims) - 1 - position))
    return factor_of


def bell_draw(own_key, dims, deviation, most, cuts=(), held_as=jnp.bfloat16):
    values = jax.random.normal(own_key, dims, jnp.float32) * deviation
    if len(cuts) > 0:
        values = block_scale(own_key, dims, cuts, -0.22, 0.18) * values
    return jnp.clip(values, min=-most, max=most).astype(held_as)


def setup_inputs(seed: int = 0, part: int = 0) -> dict:
    key_of = jax.random.split(jax.random.key(seed), 6)
    part_keys = jax.random.split(jax.random.fold_in(key_of[5], part), 6)
    query_rows = bell_draw(part_keys[0], (STEP_TOTAL, DEVICE_HEAD_SLOTS * HD), 0.1, 0.59765625, ((0, 16),))
    key_rows = bell_draw(part_keys[1], (STEP_TOTAL, DEVICE_HEAD_SLOTS * HD), 0.1, 0.59765625, ((0, 16),))
    value_rows = bell_draw(part_keys[2], (STEP_TOTAL, DEVICE_HEAD_SLOTS * HD), 0.1, 0.59765625, ((0, 16),))
    log_decay = draw_log_decay(jax.random.fold_in(jax.random.fold_in(key_of[5], part), 71), part)
    out_grad = bell_draw(part_keys[4], (STEP_TOTAL, DEVICE_HEAD_SLOTS * HD), 0.1, 0.59765625, ((0, 16),))
    return dict(query_rows=query_rows, key_rows=key_rows, value_rows=value_rows, log_decay=log_decay, out_grad=out_grad)


def decay_terms(log_decay):
    cumulative = jnp.cumsum(log_decay, axis=1)
    block_total = cumulative[:, -1:]
    length = log_decay.shape[1]
    row_index = lax.broadcasted_iota(jnp.int32, (length, length), 0)
    col_index = lax.broadcasted_iota(jnp.int32, (length, length), 1)
    causal = (col_index <= row_index)[None]
    log_gaps = cumulative[:, :, None] - cumulative[:, None, :]
    decay_mask = jnp.where(causal, jnp.exp(jnp.where(causal, log_gaps, 0.0)), 0.0)
    return cumulative, block_total, decay_mask


def forward_block(state_carry, inputs_block):
    queries, keys_local, values, decays = inputs_block
    query_wide = queries.astype(jnp.float32)
    key_wide = keys_local.astype(jnp.float32)
    value_wide = values.astype(jnp.float32)
    cumulative, block_total, decay_mask = decay_terms(decays)
    to_query = jnp.exp(cumulative).T[:, :, None]
    to_end = jnp.exp(block_total - cumulative).T[:, :, None]
    scores = jnp.einsum('thd,shd->hts', query_wide, key_wide)
    attn_weights = (scores * decay_mask).astype(jnp.bfloat16)
    state_in_rounded = state_carry.astype(jnp.bfloat16)
    inter = to_query * jnp.einsum('thd,hde->the', query_wide, state_in_rounded.astype(jnp.float32))
    intra = jnp.einsum('hts,she->the', attn_weights.astype(jnp.float32), value_wide)
    attended = (inter + intra).astype(jnp.bfloat16)
    weighted_keys = (key_wide * to_end).astype(jnp.bfloat16)
    local_state = jnp.einsum('thd,the->hde', weighted_keys.astype(jnp.float32), value_wide)
    new_state = jnp.exp(block_total[:, 0])[:, None, None] * state_carry + local_state
    return new_state, (attended, state_in_rounded)


def backward_block(grad_carry, inputs_block):
    queries, keys_local, values, decays, grads_out, state_in_rounded = inputs_block
    query_wide = queries.astype(jnp.float32)
    key_wide = keys_local.astype(jnp.float32)
    value_wide = values.astype(jnp.float32)
    grad_wide = grads_out.astype(jnp.float32)
    cumulative, block_total, decay_mask = decay_terms(decays)
    to_query = jnp.exp(cumulative).T[:, :, None]
    to_end = jnp.exp(block_total - cumulative).T[:, :, None]
    scores = jnp.einsum('thd,shd->hts', query_wide, key_wide)
    attn_weights = (scores * decay_mask).astype(jnp.bfloat16).astype(jnp.float32)
    grad_rounded = grad_carry.astype(jnp.bfloat16).astype(jnp.float32)
    state_wide = state_in_rounded.astype(jnp.float32)
    grad_scores = (jnp.einsum('the,she->hts', grad_wide, value_wide) * decay_mask).astype(jnp.bfloat16).astype(jnp.float32)
    query_grad = jnp.einsum('hts,shd->thd', grad_scores, key_wide) + to_query * jnp.einsum('the,hde->thd', grad_wide, state_wide)
    key_grad = jnp.einsum('hts,thd->shd', grad_scores, query_wide) + to_end * jnp.einsum('she,hde->shd', value_wide, grad_rounded)
    value_grad = jnp.einsum('hts,the->she', attn_weights, grad_wide) + to_end * jnp.einsum('shd,hde->she', key_wide, grad_rounded)
    scaled_queries = (query_wide * to_query).astype(jnp.bfloat16)
    local_grad = jnp.einsum('thd,the->hde', scaled_queries.astype(jnp.float32), grad_wide)
    new_grad = jnp.exp(block_total[:, 0])[:, None, None] * grad_carry + local_grad
    return new_grad, (query_grad.astype(jnp.bfloat16), key_grad.astype(jnp.bfloat16), value_grad.astype(jnp.bfloat16))


def reference(query_rows, key_rows, value_rows, log_decay, out_grad):
    blocks = STEP_TOTAL // TOK_DEV

    def split_rows(array):
        return array.reshape(blocks, TOK_DEV, DEVICE_HEAD_SLOTS, HD)

    decays = log_decay.reshape(DEVICE_HEAD_SLOTS, blocks, TOK_DEV).transpose(1, 0, 2)
    queries = split_rows(query_rows)
    keys_local = split_rows(key_rows)
    values = split_rows(value_rows)
    grads_out = split_rows(out_grad)
    start = jnp.zeros((DEVICE_HEAD_SLOTS, HD, HD), jnp.float32)
    final_state, outputs = lax.scan(forward_block, start, (queries, keys_local, values, decays))
    attended, states_in = outputs
    final_grad, grads = lax.scan(backward_block, start, (queries, keys_local, values, decays, grads_out, states_in), reverse=True)
    query_grad, key_grad, value_grad = grads

    def join_rows(array):
        return array.reshape(STEP_TOTAL, DEVICE_HEAD_SLOTS * HD)

    return (join_rows(attended), join_rows(query_grad), join_rows(key_grad), join_rows(value_grad))
```

```python
import functools

import jax
import jax.numpy as jnp
from jax import lax
from jax.experimental import pallas as pl
from jax.experimental.pallas import tpu as pltpu
from jax.sharding import PartitionSpec as P

F32 = jnp.float32
BF16 = jnp.bfloat16


def dot(a, b, a_dim, b_dim):
    return lax.dot_general(a, b, (((a_dim,), (b_dim,)), ((), ())), preferred_element_type=F32)


def kernel(
    planes,
    q_ref,
    k_ref,
    v_ref,
    g_ref,
    cum_ref,
    a_ref,
    att_ref,
    qg_ref,
    kg_ref,
    vg_ref,
    pair,
    give,
    chips,
    ztx,
    zrx,
    res,
    srx,
    dec,
    dec_send,
    dec_recv,
    pair_send,
    pair_recv,
    x_send,
    x_recv,
    z_send,
    z_recv,
    s_send,
    s_recv,
):
    n = pair.shape[1]
    width = pair.shape[-1]
    length = q_ref.shape[0]
    seq = lax.axis_index("seq")
    core = lax.rem(seq, 2)
    x = lax.rem(seq // 2, 2)
    z = seq // 4
    place = 2 * x + core
    base = 4 * z
    sibling = base + 2 * x + (1 - core)
    across = base + 2 * (1 - x) + core
    diagonal = base + 2 * (1 - x) + (1 - core)
    has_down = z > 0
    has_up = z < planes - 1

    barrier = pltpu.get_barrier_semaphore()
    for peer in (sibling, across, diagonal):
        pl.semaphore_signal(barrier, inc=1, device_id={"seq": peer})

    @pl.when(has_down)
    def _():
        pl.semaphore_signal(barrier, inc=1, device_id={"seq": seq - 4})

    @pl.when(has_up)
    def _():
        pl.semaphore_signal(barrier, inc=1, device_id={"seq": seq + 4})

    pl.semaphore_wait(barrier, 3 + has_down.astype(jnp.int32) + has_up.astype(jnp.int32))

    def remote(src, dst, send, recv, peer):
        return pltpu.make_async_remote_copy(
            src_ref=src, dst_ref=dst, send_sem=send, recv_sem=recv, device_id={"seq": peer}
        )

    def dec_copy(slot, peer):
        return remote(a_ref, dec.at[place], dec_send.at[slot], dec_recv.at[slot], peer)

    def pair_copy(j):
        return remote(give.at[j], pair.at[core, j], pair_send.at[j], pair_recv.at[j], sibling)

    def x_copy(d, j):
        return remote(
            chips.at[x, d, j], chips.at[x, d, j], x_send.at[d, j], x_recv.at[d, j], across
        )

    def z_copy(d, j):
        peer = seq + 4 if d == 0 else seq - 4
        return remote(ztx.at[d, j], zrx.at[d, j], z_send.at[d, j], z_recv.at[d, j], peer)

    def s_copy(d, j):
        return remote(
            res.at[1 - core, d, j], srx.at[d, j], s_send.at[d, j], s_recv.at[d, j], sibling
        )

    dec_copies = [dec_copy(0, sibling), dec_copy(1, across), dec_copy(2, diagonal)]
    for copy in dec_copies:
        copy.start()
    dec[place] = a_ref[...]

    row_index = lax.broadcasted_iota(jnp.int32, (length, length), 0)
    col_index = lax.broadcasted_iota(jnp.int32, (length, length), 1)

    def column(row):
        return jnp.sum(jnp.where(row_index == col_index, row, 0.0), axis=1, keepdims=True)

    def lanes(head):
        return pl.ds(pl.multiple_of(head * width, width), width)

    def decay(p, head):
        return dec[p, pl.ds(head, 1), :]

    def local_states(head, dst):
        cols = lanes(head)
        row = cum_ref[pl.ds(head, 1), :]
        col = column(row)
        total = row[:, length - 1 : length]
        weighted = (k_ref[:, cols].astype(F32) * jnp.exp(total - col)).astype(BF16)
        scaled = (q_ref[:, cols].astype(F32) * jnp.exp(col)).astype(BF16)
        dst[0] = dot(weighted, v_ref[:, cols], 0, 0)
        dst[1] = dot(scaled, g_ref[:, cols], 0, 0)

    def first(i, carry):
        @pl.when(i < n)
        def _():
            local_states((1 - core) * n + i, give.at[i])
            pair_copy(i).start()
            local_states(core * n + i, pair.at[core, i])

        @pl.when(i == 1)
        def _():
            dec_copies[0].wait_recv()

        @pl.when(i >= 1)
        def _():
            j = i - 1
            head = core * n + j
            pair_copy(j).wait_recv()
            chips[x, 0, j] = decay(2 * x + 1, head) * pair[0, j, 0] + pair[1, j, 0]
            x_copy(0, j).start()
            chips[x, 1, j] = decay(2 * x, head) * pair[1, j, 1] + pair[0, j, 1]
            x_copy(1, j).start()

        return carry

    lax.fori_loop(0, n + 1, first, 0)
    dec_copies[1].wait_recv()
    dec_copies[2].wait_recv()

    @pl.when(jnp.logical_not(has_down))
    def _():
        zrx[0] = jnp.zeros(zrx.shape[1:], F32)

    @pl.when(jnp.logical_not(has_up))
    def _():
        zrx[1] = jnp.zeros(zrx.shape[1:], F32)

    def outputs(head, state, grad):
        cols = lanes(head)
        q, k, v, g = q_ref[:, cols], k_ref[:, cols], v_ref[:, cols], g_ref[:, cols]
        row = cum_ref[pl.ds(head, 1), :]
        col = column(row)
        total = row[:, length - 1 : length]
        causal = col_index <= row_index
        mask = jnp.where(causal, jnp.exp(jnp.where(causal, col - row, 0.0)), 0.0)
        weights = (dot(q, k, 1, 1) * mask).astype(BF16)
        scores = (dot(g, v, 1, 1) * mask).astype(BF16)
        to_query = jnp.exp(col)
        to_end = jnp.exp(total - col)
        state = state.astype(BF16)
        grad = grad.astype(BF16)
        att_ref[:, cols] = (dot(weights, v, 1, 0) + to_query * dot(q, state, 1, 0)).astype(BF16)
        qg_ref[:, cols] = (dot(scores, k, 1, 0) + to_query * dot(g, state, 1, 1)).astype(BF16)
        kg_ref[:, cols] = (dot(scores, q, 0, 0) + to_end * dot(v, grad, 1, 1)).astype(BF16)
        vg_ref[:, cols] = (dot(weights, g, 0, 0) + to_end * dot(k, grad, 1, 0)).astype(BF16)

    lag = jnp.maximum(z, planes - 1 - z) + 1

    def second(t, carry):
        jf = t - z

        @pl.when(jnp.logical_and(jf >= 0, jf < n))
        def _():
            head = core * n + jf
            a00, a01 = decay(0, head), decay(1, head)
            a10, a11 = decay(2, head), decay(3, head)
            x_copy(0, jf).wait_recv()

            @pl.when(has_down)
            def _():
                z_copy(0, jf).wait_recv()

            before = zrx[0, jf]
            middle = (a00 * a01) * before + chips[0, 0, jf]

            @pl.when(has_up)
            def _():
                ztx[0, jf] = (a10 * a11) * middle + chips[1, 0, jf]
                z_copy(0, jf).start()

            into = jnp.where(x == 0, before, middle)
            res[0, 0, jf] = into
            res[1, 0, jf] = decay(2 * x, head) * into + pair[0, jf, 0]
            s_copy(0, jf).start()

        jb = t - (planes - 1 - z)

        @pl.when(jnp.logical_and(jb >= 0, jb < n))
        def _():
            head = core * n + jb
            a00, a01 = decay(0, head), decay(1, head)
            a10, a11 = decay(2, head), decay(3, head)
            x_copy(1, jb).wait_recv()

            @pl.when(has_up)
            def _():
                z_copy(1, jb).wait_recv()

            after = zrx[1, jb]
            middle = (a10 * a11) * after + chips[1, 1, jb]

            @pl.when(has_down)
            def _():
                ztx[1, jb] = (a00 * a01) * middle + chips[0, 1, jb]
                z_copy(1, jb).start()

            into = jnp.where(x == 1, after, middle)
            res[1, 1, jb] = into
            res[0, 1, jb] = decay(2 * x + 1, head) * into + pair[1, jb, 1]
            s_copy(1, jb).start()

        jo = t - lag

        @pl.when(jnp.logical_and(jo >= 0, jo < n))
        def _():
            outputs(core * n + jo, res[core, 0, jo], res[core, 1, jo])
            s_copy(0, jo).wait_recv()
            s_copy(1, jo).wait_recv()
            outputs((1 - core) * n + jo, srx[0, jo], srx[1, jo])

        return carry

    lax.fori_loop(0, n + planes, second, 0)

    for copy in dec_copies:
        copy.wait_send()

    def drain(j, carry):
        pair_copy(j).wait_send()
        for d in (0, 1):
            x_copy(d, j).wait_send()
            s_copy(d, j).wait_send()

        @pl.when(has_up)
        def _():
            z_copy(0, j).wait_send()

        @pl.when(has_down)
        def _():
            z_copy(1, j).wait_send()

        return carry

    lax.fori_loop(0, n, drain, 0)


def on_device(planes, query_rows, key_rows, value_rows, log_decay, out_grad):
    heads = log_decay.shape[0]
    width = query_rows.shape[1] // heads
    n = heads // 2
    cumulative = jnp.cumsum(log_decay, axis=1)
    carried = jnp.broadcast_to(jnp.exp(cumulative[:, -1:]), (heads, width))
    square = (width, width)
    dma = pltpu.SemaphoreType.DMA
    shape = jax.ShapeDtypeStruct(query_rows.shape, BF16)
    return pl.pallas_call(
        functools.partial(kernel, planes),
        out_shape=(shape,) * 4,
        in_specs=[pl.BlockSpec(memory_space=pltpu.VMEM)] * 6,
        out_specs=(pl.BlockSpec(memory_space=pltpu.VMEM),) * 4,
        scratch_shapes=[
            pltpu.VMEM((2, n, 2) + square, F32),
            pltpu.VMEM((n, 2) + square, F32),
            pltpu.VMEM((2, 2, n) + square, F32),
            pltpu.VMEM((2, n) + square, F32),
            pltpu.VMEM((2, n) + square, F32),
            pltpu.VMEM((2, 2, n) + square, F32),
            pltpu.VMEM((2, n) + square, F32),
            pltpu.VMEM((4, heads, width), F32),
            dma((3,)),
            dma((3,)),
            dma((n,)),
            dma((n,)),
            dma((2, n)),
            dma((2, n)),
            dma((2, n)),
            dma((2, n)),
            dma((2, n)),
            dma((2, n)),
        ],
        compiler_params=pltpu.CompilerParams(
            collective_id=0, has_side_effects=True, vmem_limit_bytes=48 * 1024 * 1024
        ),
    )(query_rows, key_rows, value_rows, out_grad, cumulative, carried)


def solution(mesh):
    rows = P(("grp", "seq"), None)
    in_specs = (rows, rows, rows, P(None, ("grp", "seq")), rows)
    return jax.shard_map(
        functools.partial(on_device, mesh.shape["seq"] // 4),
        mesh=mesh,
        in_specs=in_specs,
        out_specs=(rows,) * 4,
        check_vma=False,
    )
```

```python
import functools

import jax
import jax.numpy as jnp
from jax import lax
from jax.experimental import pallas as pl
from jax.experimental.pallas import tpu as pltpu
from jax.sharding import PartitionSpec as P

F32 = jnp.float32
BF16 = jnp.bfloat16
HOP_SLOTS = 2


def dot(a, b, a_dim, b_dim):
    return lax.dot_general(a, b, (((a_dim,), (b_dim,)), ((), ())), preferred_element_type=F32)


def kernel(
    planes,
    q_in,
    k_in,
    v_in,
    g_in,
    log_ref,
    att_out,
    qg_out,
    kg_out,
    vg_out,
    rows,
    outs,
    cum_ref,
    pair,
    give,
    chips,
    ztx,
    zrx,
    res,
    srx,
    dec,
    in_sem,
    out_sem,
    dec_send,
    dec_recv,
    pair_send,
    pair_recv,
    x_send,
    x_recv,
    z_send,
    z_recv,
    s_send,
    s_recv,
):
    n = pair.shape[1]
    width = pair.shape[-1]
    length = rows.shape[1]
    q_ref, k_ref, v_ref, g_ref = (rows.at[i] for i in range(4))
    seq = lax.axis_index("seq")
    core = lax.rem(seq, 2)
    x = lax.rem(seq // 2, 2)
    z = seq // 4
    place = 2 * x + core
    base = 4 * z
    sibling = base + 2 * x + (1 - core)
    across = base + 2 * (1 - x) + core
    diagonal = base + 2 * (1 - x) + (1 - core)
    has_down = z > 0
    has_up = z < planes - 1

    loads = [
        pltpu.make_async_copy(src, rows.at[i], in_sem.at[i])
        for i, src in enumerate((q_in, k_in, v_in, g_in))
    ]
    for load in loads:
        load.start()

    barrier = pltpu.get_barrier_semaphore()
    for peer in (sibling, across, diagonal):
        pl.semaphore_signal(barrier, inc=1, device_id={"seq": peer})

    @pl.when(has_down)
    def _():
        pl.semaphore_signal(barrier, inc=1, device_id={"seq": seq - 4})

    @pl.when(has_up)
    def _():
        pl.semaphore_signal(barrier, inc=1, device_id={"seq": seq + 4})

    row_index = lax.broadcasted_iota(jnp.int32, (length, length), 0)
    col_index = lax.broadcasted_iota(jnp.int32, (length, length), 1)
    cum_ref[...] = lax.dot_general(
        log_ref[...],
        (row_index <= col_index).astype(F32),
        (((1,), (0,)), ((), ())),
        precision=lax.Precision.HIGHEST,
        preferred_element_type=F32,
    )
    dec[place] = jnp.broadcast_to(jnp.exp(cum_ref[:, length - 1 : length]), dec.shape[1:])

    pl.semaphore_wait(barrier, 3 + has_down.astype(jnp.int32) + has_up.astype(jnp.int32))

    def remote(src, dst, send, recv, peer):
        return pltpu.make_async_remote_copy(
            src_ref=src, dst_ref=dst, send_sem=send, recv_sem=recv, device_id={"seq": peer}
        )

    def dec_copy(slot, peer):
        return remote(dec.at[place], dec.at[place], dec_send.at[slot], dec_recv.at[slot], peer)

    def pair_copy(j):
        return remote(give.at[j], pair.at[core, j], pair_send.at[j], pair_recv.at[j], sibling)

    def x_copy(d, j):
        return remote(
            chips.at[x, d, j], chips.at[x, d, j], x_send.at[d, j], x_recv.at[d, j], across
        )

    def z_copy(d, j):
        peer = seq + 4 if d == 0 else seq - 4
        return remote(ztx.at[d, j], zrx.at[d, j], z_send.at[d, j], z_recv.at[d, j], peer)

    def s_copy(d, j):
        return remote(
            res.at[1 - core, d, j], srx.at[d, j], s_send.at[d, j], s_recv.at[d, j], sibling
        )

    dec_copies = [dec_copy(0, sibling), dec_copy(1, across), dec_copy(2, diagonal)]
    for copy in dec_copies:
        copy.start()
    for load in loads:
        load.wait()

    def column(row):
        return jnp.sum(jnp.where(row_index == col_index, row, 0.0), axis=1, keepdims=True)

    def lanes(head):
        return pl.ds(pl.multiple_of(head * width, width), width)

    def decay(p, head):
        return dec[p, pl.ds(head, 1), :]

    def local_states(head, dst):
        cols = lanes(head)
        row = cum_ref[pl.ds(head, 1), :]
        col = column(row)
        total = row[:, length - 1 : length]
        weighted = (k_ref[:, cols].astype(F32) * jnp.exp(total - col)).astype(BF16)
        scaled = (q_ref[:, cols].astype(F32) * jnp.exp(col)).astype(BF16)
        dst[0] = dot(weighted, v_ref[:, cols], 0, 0)
        dst[1] = dot(scaled, g_ref[:, cols], 0, 0)

    def first(i, carry):
        @pl.when(i < n)
        def _():
            local_states((1 - core) * n + i, give.at[i])
            pair_copy(i).start()
            local_states(core * n + i, pair.at[core, i])

        @pl.when(i == 1)
        def _():
            dec_copies[0].wait_recv()

        @pl.when(i >= 1)
        def _():
            j = i - 1
            head = core * n + j
            pair_copy(j).wait_recv()
            chips[x, 0, j] = decay(2 * x + 1, head) * pair[0, j, 0] + pair[1, j, 0]
            x_copy(0, j).start()
            chips[x, 1, j] = decay(2 * x, head) * pair[1, j, 1] + pair[0, j, 1]
            x_copy(1, j).start()

        return carry

    lax.fori_loop(0, n + 1, first, 0)
    dec_copies[1].wait_recv()
    dec_copies[2].wait_recv()

    @pl.when(jnp.logical_not(has_down))
    def _():
        zrx[0] = jnp.zeros(zrx.shape[1:], F32)

    @pl.when(jnp.logical_not(has_up))
    def _():
        zrx[1] = jnp.zeros(zrx.shape[1:], F32)

    results = (att_out, qg_out, kg_out, vg_out)

    def outputs(head, state, grad):
        cols = lanes(head)
        q, k, v, g = q_ref[:, cols], k_ref[:, cols], v_ref[:, cols], g_ref[:, cols]
        row = cum_ref[pl.ds(head, 1), :]
        col = column(row)
        total = row[:, length - 1 : length]
        causal = col_index <= row_index
        mask = jnp.where(causal, jnp.exp(jnp.where(causal, col - row, 0.0)), 0.0)
        weights = (dot(q, k, 1, 1) * mask).astype(BF16)
        scores = (dot(g, v, 1, 1) * mask).astype(BF16)
        to_query = jnp.exp(col)
        to_end = jnp.exp(total - col)
        state = state.astype(BF16)
        grad = grad.astype(BF16)
        outs[0, :, cols] = (dot(weights, v, 1, 0) + to_query * dot(q, state, 1, 0)).astype(BF16)
        outs[1, :, cols] = (dot(scores, k, 1, 0) + to_query * dot(g, state, 1, 1)).astype(BF16)
        outs[2, :, cols] = (dot(scores, q, 0, 0) + to_end * dot(v, grad, 1, 1)).astype(BF16)
        outs[3, :, cols] = (dot(weights, g, 0, 0) + to_end * dot(k, grad, 1, 0)).astype(BF16)
        for i, dst in enumerate(results):
            pltpu.make_async_copy(outs.at[i, :, cols], dst.at[:, cols], out_sem.at[i]).start()

    lag = HOP_SLOTS * jnp.maximum(z, planes - 1 - z) + 1

    def second(t, carry):
        jf = t - HOP_SLOTS * z

        @pl.when(jnp.logical_and(jf >= 0, jf < n))
        def _():
            head = core * n + jf
            a00, a01 = decay(0, head), decay(1, head)
            a10, a11 = decay(2, head), decay(3, head)
            x_copy(0, jf).wait_recv()

            @pl.when(has_down)
            def _():
                z_copy(0, jf).wait_recv()

            before = zrx[0, jf]
            middle = (a00 * a01) * before + chips[0, 0, jf]

            @pl.when(has_up)
            def _():
                ztx[0, jf] = (a10 * a11) * middle + chips[1, 0, jf]
                z_copy(0, jf).start()

            into = jnp.where(x == 0, before, middle)
            res[0, 0, jf] = into
            res[1, 0, jf] = decay(2 * x, head) * into + pair[0, jf, 0]
            s_copy(0, jf).start()

        jb = t - HOP_SLOTS * (planes - 1 - z)

        @pl.when(jnp.logical_and(jb >= 0, jb < n))
        def _():
            head = core * n + jb
            a00, a01 = decay(0, head), decay(1, head)
            a10, a11 = decay(2, head), decay(3, head)
            x_copy(1, jb).wait_recv()

            @pl.when(has_up)
            def _():
                z_copy(1, jb).wait_recv()

            after = zrx[1, jb]
            middle = (a10 * a11) * after + chips[1, 1, jb]

            @pl.when(has_down)
            def _():
                ztx[1, jb] = (a00 * a01) * middle + chips[0, 1, jb]
                z_copy(1, jb).start()

            into = jnp.where(x == 1, after, middle)
            res[1, 1, jb] = into
            res[0, 1, jb] = decay(2 * x + 1, head) * into + pair[1, jb, 1]
            s_copy(1, jb).start()

        jo = t - lag

        @pl.when(jnp.logical_and(jo >= 0, jo < n))
        def _():
            outputs(core * n + jo, res[core, 0, jo], res[core, 1, jo])
            s_copy(0, jo).wait_recv()
            s_copy(1, jo).wait_recv()
            outputs((1 - core) * n + jo, srx[0, jo], srx[1, jo])

        return carry

    lax.fori_loop(0, n + HOP_SLOTS * (planes - 1) + 1, second, 0)

    for i, dst in enumerate(results):
        pltpu.make_async_copy(outs.at[i], dst, out_sem.at[i]).wait()
    for copy in dec_copies:
        copy.wait_send()

    def drain(j, carry):
        pair_copy(j).wait_send()
        for d in (0, 1):
            x_copy(d, j).wait_send()
            s_copy(d, j).wait_send()

        @pl.when(has_up)
        def _():
            z_copy(0, j).wait_send()

        @pl.when(has_down)
        def _():
            z_copy(1, j).wait_send()

        return carry

    lax.fori_loop(0, n, drain, 0)


def on_device(planes, query_rows, key_rows, value_rows, log_decay, out_grad):
    heads = log_decay.shape[0]
    width = query_rows.shape[1] // heads
    n = heads // 2
    square = (width, width)
    dma = pltpu.SemaphoreType.DMA
    shape = jax.ShapeDtypeStruct(query_rows.shape, BF16)
    return pl.pallas_call(
        functools.partial(kernel, planes),
        out_shape=(shape,) * 4,
        in_specs=[pl.BlockSpec(memory_space=pl.ANY)] * 4
        + [pl.BlockSpec(memory_space=pltpu.VMEM)],
        out_specs=(pl.BlockSpec(memory_space=pl.ANY),) * 4,
        scratch_shapes=[
            pltpu.VMEM((4,) + query_rows.shape, BF16),
            pltpu.VMEM((4,) + query_rows.shape, BF16),
            pltpu.VMEM(log_decay.shape, F32),
            pltpu.VMEM((2, n, 2) + square, F32),
            pltpu.VMEM((n, 2) + square, F32),
            pltpu.VMEM((2, 2, n) + square, F32),
            pltpu.VMEM((2, n) + square, F32),
            pltpu.VMEM((2, n) + square, F32),
            pltpu.VMEM((2, 2, n) + square, F32),
            pltpu.VMEM((2, n) + square, F32),
            pltpu.VMEM((4, heads, width), F32),
            dma((4,)),
            dma((4,)),
            dma((3,)),
            dma((3,)),
            dma((n,)),
            dma((n,)),
            dma((2, n)),
            dma((2, n)),
            dma((2, n)),
            dma((2, n)),
            dma((2, n)),
            dma((2, n)),
        ],
        compiler_params=pltpu.CompilerParams(
            collective_id=0, has_side_effects=True, vmem_limit_bytes=48 * 1024 * 1024
        ),
    )(query_rows, key_rows, value_rows, out_grad, log_decay)


def solution(mesh):
    rows = P(("grp", "seq"), None)
    in_specs = (rows, rows, rows, P(None, ("grp", "seq")), rows)
    return jax.shard_map(
        functools.partial(on_device, mesh.shape["seq"] // 4),
        mesh=mesh,
        in_specs=in_specs,
        out_specs=(rows,) * 4,
        check_vma=False,
    )
```

```python
import functools

import jax
import jax.numpy as jnp
from jax import lax
from jax.experimental import pallas as pl
from jax.experimental.pallas import tpu as pltpu
from jax.sharding import PartitionSpec as P

F32 = jnp.float32
BF16 = jnp.bfloat16
HOP_SLOTS = 3


def dot(a, b, a_dim, b_dim):
    return lax.dot_general(a, b, (((a_dim,), (b_dim,)), ((), ())), preferred_element_type=F32)


def kernel(
    planes,
    q_in,
    k_in,
    v_in,
    g_in,
    log_ref,
    att_out,
    qg_out,
    kg_out,
    vg_out,
    rows,
    outs,
    cum_ref,
    pair,
    give,
    chips,
    ztx,
    zrx,
    res,
    srx,
    dec,
    in_sem,
    out_sem,
    dec_send,
    dec_recv,
    pair_send,
    pair_recv,
    x_send,
    x_recv,
    z_send,
    z_recv,
    s_send,
    s_recv,
):
    n = pair.shape[1]
    width = pair.shape[-1]
    length = rows.shape[1]
    q_ref, k_ref, v_ref, g_ref = (rows.at[i] for i in range(4))
    seq = lax.axis_index("seq")
    core = lax.rem(seq, 2)
    x = lax.rem(seq // 2, 2)
    z = seq // 4
    place = 2 * x + core
    base = 4 * z
    sibling = base + 2 * x + (1 - core)
    across = base + 2 * (1 - x) + core
    diagonal = base + 2 * (1 - x) + (1 - core)
    has_down = z > 0
    has_up = z < planes - 1

    loads = [
        pltpu.make_async_copy(src, rows.at[i], in_sem.at[i])
        for i, src in enumerate((q_in, k_in, v_in, g_in))
    ]
    for load in loads:
        load.start()

    barrier = pltpu.get_barrier_semaphore()
    for peer in (sibling, across, diagonal):
        pl.semaphore_signal(barrier, inc=1, device_id={"seq": peer})

    @pl.when(has_down)
    def _():
        pl.semaphore_signal(barrier, inc=1, device_id={"seq": seq - 4})

    @pl.when(has_up)
    def _():
        pl.semaphore_signal(barrier, inc=1, device_id={"seq": seq + 4})

    row_index = lax.broadcasted_iota(jnp.int32, (length, length), 0)
    col_index = lax.broadcasted_iota(jnp.int32, (length, length), 1)
    cum_ref[...] = lax.dot_general(
        log_ref[...],
        (row_index <= col_index).astype(F32),
        (((1,), (0,)), ((), ())),
        precision=lax.Precision.HIGHEST,
        preferred_element_type=F32,
    )
    dec[place] = jnp.broadcast_to(jnp.exp(cum_ref[:, length - 1 : length]), dec.shape[1:])

    pl.semaphore_wait(barrier, 3 + has_down.astype(jnp.int32) + has_up.astype(jnp.int32))

    def remote(src, dst, send, recv, peer):
        return pltpu.make_async_remote_copy(
            src_ref=src, dst_ref=dst, send_sem=send, recv_sem=recv, device_id={"seq": peer}
        )

    def dec_copy(slot, peer):
        return remote(dec.at[place], dec.at[place], dec_send.at[slot], dec_recv.at[slot], peer)

    def pair_copy(j):
        return remote(give.at[j], pair.at[core, j], pair_send.at[j], pair_recv.at[j], sibling)

    def x_copy(d, j):
        return remote(
            chips.at[x, d, j], chips.at[x, d, j], x_send.at[d, j], x_recv.at[d, j], across
        )

    def z_copy(d, j):
        peer = seq + 4 if d == 0 else seq - 4
        return remote(ztx.at[d, j], zrx.at[d, j], z_send.at[d, j], z_recv.at[d, j], peer)

    def s_copy(d, j):
        return remote(
            res.at[1 - core, d, j], srx.at[d, j], s_send.at[d, j], s_recv.at[d, j], sibling
        )

    dec_copies = [dec_copy(0, sibling), dec_copy(1, across), dec_copy(2, diagonal)]
    for copy in dec_copies:
        copy.start()
    for load in loads:
        load.wait()

    def column(row):
        return jnp.sum(jnp.where(row_index == col_index, row, 0.0), axis=1, keepdims=True)

    def lanes(head):
        return pl.ds(pl.multiple_of(head * width, width), width)

    def decay(p, head):
        return dec[p, pl.ds(head, 1), :]

    def local_states(head, dst):
        cols = lanes(head)
        row = cum_ref[pl.ds(head, 1), :]
        col = column(row)
        total = row[:, length - 1 : length]
        weighted = (k_ref[:, cols].astype(F32) * jnp.exp(total - col)).astype(BF16)
        scaled = (q_ref[:, cols].astype(F32) * jnp.exp(col)).astype(BF16)
        dst[0] = dot(weighted, v_ref[:, cols], 0, 0)
        dst[1] = dot(scaled, g_ref[:, cols], 0, 0)

    lead = jnp.where(2 * z <= planes - 1, 0, 1)
    offset = HOP_SLOTS * jnp.abs(planes - 1 - 2 * z)

    def first(i, carry):
        @pl.when(i < n)
        def _():
            local_states((1 - core) * n + i, give.at[i])
            pair_copy(i).start()
            local_states(core * n + i, pair.at[core, i])

        @pl.when(i == 1)
        def _():
            dec_copies[0].wait_recv()

        @pl.when(i >= 1)
        def _():
            j = i - 1
            head = core * n + j
            pair_copy(j).wait_recv()
            chips[x, 0, j] = decay(2 * x + 1, head) * pair[0, j, 0] + pair[1, j, 0]
            chips[x, 1, j] = decay(2 * x, head) * pair[1, j, 1] + pair[0, j, 1]
            x_copy(lead, j).start()

            @pl.when(j >= offset)
            def _():
                x_copy(1 - lead, j - offset).start()

        return carry

    lax.fori_loop(0, n + 1, first, 0)

    def rest(j, carry):
        @pl.when(j + offset >= n)
        def _():
            x_copy(1 - lead, j).start()

        return carry

    lax.fori_loop(0, n, rest, 0)
    dec_copies[1].wait_recv()
    dec_copies[2].wait_recv()

    @pl.when(jnp.logical_not(has_down))
    def _():
        zrx[0] = jnp.zeros(zrx.shape[1:], F32)

    @pl.when(jnp.logical_not(has_up))
    def _():
        zrx[1] = jnp.zeros(zrx.shape[1:], F32)

    results = (att_out, qg_out, kg_out, vg_out)

    def outputs(head, state, grad):
        cols = lanes(head)
        q, k, v, g = q_ref[:, cols], k_ref[:, cols], v_ref[:, cols], g_ref[:, cols]
        row = cum_ref[pl.ds(head, 1), :]
        col = column(row)
        total = row[:, length - 1 : length]
        causal = col_index <= row_index
        mask = jnp.where(causal, jnp.exp(jnp.where(causal, col - row, 0.0)), 0.0)
        weights = (dot(q, k, 1, 1) * mask).astype(BF16)
        scores = (dot(g, v, 1, 1) * mask).astype(BF16)
        to_query = jnp.exp(col)
        to_end = jnp.exp(total - col)
        state = state.astype(BF16)
        grad = grad.astype(BF16)
        outs[0, :, cols] = (dot(weights, v, 1, 0) + to_query * dot(q, state, 1, 0)).astype(BF16)
        outs[1, :, cols] = (dot(scores, k, 1, 0) + to_query * dot(g, state, 1, 1)).astype(BF16)
        outs[2, :, cols] = (dot(scores, q, 0, 0) + to_end * dot(v, grad, 1, 1)).astype(BF16)
        outs[3, :, cols] = (dot(weights, g, 0, 0) + to_end * dot(k, grad, 1, 0)).astype(BF16)
        for i, dst in enumerate(results):
            pltpu.make_async_copy(outs.at[i, :, cols], dst.at[:, cols], out_sem.at[i]).start()

    lag = HOP_SLOTS * jnp.maximum(z, planes - 1 - z) + 1

    def second(t, carry):
        jf = t - HOP_SLOTS * z

        @pl.when(jnp.logical_and(jf >= 0, jf < n))
        def _():
            head = core * n + jf
            a00, a01 = decay(0, head), decay(1, head)
            a10, a11 = decay(2, head), decay(3, head)
            x_copy(0, jf).wait_recv()

            @pl.when(has_down)
            def _():
                z_copy(0, jf).wait_recv()

            before = zrx[0, jf]
            middle = (a00 * a01) * before + chips[0, 0, jf]

            @pl.when(has_up)
            def _():
                ztx[0, jf] = (a10 * a11) * middle + chips[1, 0, jf]
                z_copy(0, jf).start()

            into = jnp.where(x == 0, before, middle)
            res[0, 0, jf] = into
            res[1, 0, jf] = decay(2 * x, head) * into + pair[0, jf, 0]
            s_copy(0, jf).start()

        jb = t - HOP_SLOTS * (planes - 1 - z)

        @pl.when(jnp.logical_and(jb >= 0, jb < n))
        def _():
            head = core * n + jb
            a00, a01 = decay(0, head), decay(1, head)
            a10, a11 = decay(2, head), decay(3, head)
            x_copy(1, jb).wait_recv()

            @pl.when(has_up)
            def _():
                z_copy(1, jb).wait_recv()

            after = zrx[1, jb]
            middle = (a10 * a11) * after + chips[1, 1, jb]

            @pl.when(has_down)
            def _():
                ztx[1, jb] = (a00 * a01) * middle + chips[0, 1, jb]
                z_copy(1, jb).start()

            into = jnp.where(x == 1, after, middle)
            res[1, 1, jb] = into
            res[0, 1, jb] = decay(2 * x + 1, head) * into + pair[1, jb, 1]
            s_copy(1, jb).start()

        jo = t - lag

        @pl.when(jnp.logical_and(jo >= 0, jo < n))
        def _():
            outputs(core * n + jo, res[core, 0, jo], res[core, 1, jo])
            s_copy(0, jo).wait_recv()
            s_copy(1, jo).wait_recv()
            outputs((1 - core) * n + jo, srx[0, jo], srx[1, jo])

        return carry

    lax.fori_loop(0, n + HOP_SLOTS * (planes - 1) + 1, second, 0)

    for i, dst in enumerate(results):
        pltpu.make_async_copy(outs.at[i], dst, out_sem.at[i]).wait()
    for copy in dec_copies:
        copy.wait_send()

    def drain(j, carry):
        pair_copy(j).wait_send()
        for d in (0, 1):
            x_copy(d, j).wait_send()
            s_copy(d, j).wait_send()

        @pl.when(has_up)
        def _():
            z_copy(0, j).wait_send()

        @pl.when(has_down)
        def _():
            z_copy(1, j).wait_send()

        return carry

    lax.fori_loop(0, n, drain, 0)


def on_device(planes, query_rows, key_rows, value_rows, log_decay, out_grad):
    heads = log_decay.shape[0]
    width = query_rows.shape[1] // heads
    n = heads // 2
    square = (width, width)
    dma = pltpu.SemaphoreType.DMA
    shape = jax.ShapeDtypeStruct(query_rows.shape, BF16)
    return pl.pallas_call(
        functools.partial(kernel, planes),
        out_shape=(shape,) * 4,
        in_specs=[pl.BlockSpec(memory_space=pl.ANY)] * 4
        + [pl.BlockSpec(memory_space=pltpu.VMEM)],
        out_specs=(pl.BlockSpec(memory_space=pl.ANY),) * 4,
        scratch_shapes=[
            pltpu.VMEM((4,) + query_rows.shape, BF16),
            pltpu.VMEM((4,) + query_rows.shape, BF16),
            pltpu.VMEM(log_decay.shape, F32),
            pltpu.VMEM((2, n, 2) + square, F32),
            pltpu.VMEM((n, 2) + square, F32),
            pltpu.VMEM((2, 2, n) + square, F32),
            pltpu.VMEM((2, n) + square, F32),
            pltpu.VMEM((2, n) + square, F32),
            pltpu.VMEM((2, 2, n) + square, F32),
            pltpu.VMEM((2, n) + square, F32),
            pltpu.VMEM((4, heads, width), F32),
            dma((4,)),
            dma((4,)),
            dma((3,)),
            dma((3,)),
            dma((n,)),
            dma((n,)),
            dma((2, n)),
            dma((2, n)),
            dma((2, n)),
            dma((2, n)),
            dma((2, n)),
            dma((2, n)),
        ],
        compiler_params=pltpu.CompilerParams(
            collective_id=0, has_side_effects=True, vmem_limit_bytes=48 * 1024 * 1024
        ),
    )(query_rows, key_rows, value_rows, out_grad, log_decay)


def solution(mesh):
    rows = P(("grp", "seq"), None)
    in_specs = (rows, rows, rows, P(None, ("grp", "seq")), rows)
    return jax.shard_map(
        functools.partial(on_device, mesh.shape["seq"] // 4),
        mesh=mesh,
        in_specs=in_specs,
        out_specs=(rows,) * 4,
        check_vma=False,
    )
```

```python
import functools

import jax
import jax.numpy as jnp
from jax import lax
from jax.experimental import pallas as pl
from jax.experimental.pallas import tpu as pltpu
from jax.sharding import PartitionSpec as P

F32 = jnp.float32
BF16 = jnp.bfloat16
HOP_SLOTS = 3


def dot(a, b, a_dim, b_dim):
    return lax.dot_general(a, b, (((a_dim,), (b_dim,)), ((), ())), preferred_element_type=F32)


def kernel(
    planes,
    q_in,
    k_in,
    v_in,
    g_in,
    log_ref,
    att_out,
    qg_out,
    kg_out,
    vg_out,
    rows,
    outs,
    cum_ref,
    pair,
    give,
    chips,
    ztx,
    zrx,
    res,
    srx,
    dec,
    in_sem,
    out_sem,
    dec_send,
    dec_recv,
    pair_send,
    pair_recv,
    x_send,
    x_recv,
    z_send,
    z_recv,
    s_send,
    s_recv,
):
    n = pair.shape[1]
    width = pair.shape[-1]
    length = rows.shape[1]
    q_ref, k_ref, v_ref, g_ref = (rows.at[i] for i in range(4))
    seq = lax.axis_index("seq")
    core = lax.rem(seq, 2)
    x = lax.rem(seq // 2, 2)
    z = seq // 4
    place = 2 * x + core
    base = 4 * z
    sibling = base + 2 * x + (1 - core)
    across = base + 2 * (1 - x) + core
    diagonal = base + 2 * (1 - x) + (1 - core)
    has_down = z > 0
    has_up = z < planes - 1

    loads = [
        pltpu.make_async_copy(src, rows.at[i], in_sem.at[i])
        for i, src in enumerate((q_in, k_in, v_in, g_in))
    ]
    for load in loads:
        load.start()

    barrier = pltpu.get_barrier_semaphore()
    for peer in (sibling, across, diagonal):
        pl.semaphore_signal(barrier, inc=1, device_id={"seq": peer})

    @pl.when(has_down)
    def _():
        pl.semaphore_signal(barrier, inc=1, device_id={"seq": seq - 4})

    @pl.when(has_up)
    def _():
        pl.semaphore_signal(barrier, inc=1, device_id={"seq": seq + 4})

    row_index = lax.broadcasted_iota(jnp.int32, (length, length), 0)
    col_index = lax.broadcasted_iota(jnp.int32, (length, length), 1)
    cum_ref[...] = lax.dot_general(
        log_ref[...],
        (row_index <= col_index).astype(F32),
        (((1,), (0,)), ((), ())),
        precision=lax.Precision.HIGHEST,
        preferred_element_type=F32,
    )
    dec[place] = jnp.broadcast_to(jnp.exp(cum_ref[:, length - 1 : length]), dec.shape[1:])

    pl.semaphore_wait(barrier, 3 + has_down.astype(jnp.int32) + has_up.astype(jnp.int32))

    def remote(src, dst, send, recv, peer):
        return pltpu.make_async_remote_copy(
            src_ref=src, dst_ref=dst, send_sem=send, recv_sem=recv, device_id={"seq": peer}
        )

    def dec_copy(slot, peer):
        return remote(dec.at[place], dec.at[place], dec_send.at[slot], dec_recv.at[slot], peer)

    def pair_copy(j):
        return remote(give.at[j], pair.at[core, j], pair_send.at[j], pair_recv.at[j], sibling)

    def x_copy(d, j):
        return remote(
            chips.at[x, d, j], chips.at[x, d, j], x_send.at[d, j], x_recv.at[d, j], across
        )

    def z_copy(d, j):
        peer = seq + 4 if d == 0 else seq - 4
        return remote(ztx.at[d, j], zrx.at[d, j], z_send.at[d, j], z_recv.at[d, j], peer)

    def s_copy(d, j):
        return remote(
            res.at[1 - core, d, j], srx.at[d, j], s_send.at[d, j], s_recv.at[d, j], sibling
        )

    dec_copies = [dec_copy(0, sibling), dec_copy(1, across), dec_copy(2, diagonal)]
    for copy in dec_copies:
        copy.start()
    for load in loads:
        load.wait()

    def column(row):
        return jnp.sum(jnp.where(row_index == col_index, row, 0.0), axis=1, keepdims=True)

    def lanes(head):
        return pl.ds(pl.multiple_of(head * width, width), width)

    def decay(p, head):
        return dec[p, pl.ds(head, 1), :]

    def local_states(head, dst):
        cols = lanes(head)
        row = cum_ref[pl.ds(head, 1), :]
        col = column(row)
        total = row[:, length - 1 : length]
        weighted = (k_ref[:, cols].astype(F32) * jnp.exp(total - col)).astype(BF16)
        scaled = (q_ref[:, cols].astype(F32) * jnp.exp(col)).astype(BF16)
        dst[0] = dot(weighted, v_ref[:, cols], 0, 0)
        dst[1] = dot(scaled, g_ref[:, cols], 0, 0)

    lead = jnp.where(2 * z <= planes - 1, 0, 1)
    offset = HOP_SLOTS * jnp.abs(planes - 1 - 2 * z)

    def first(i, carry):
        @pl.when(i < n)
        def _():
            local_states((1 - core) * n + i, give.at[i])
            pair_copy(i).start()

        @pl.when(i == 1)
        def _():
            dec_copies[0].wait_recv()

        @pl.when(i >= 1)
        def _():
            j = i - 1
            head = core * n + j
            pair_copy(j).wait_recv()
            chips[x, 0, j] = decay(2 * x + 1, head) * pair[0, j, 0] + pair[1, j, 0]
            chips[x, 1, j] = decay(2 * x, head) * pair[1, j, 1] + pair[0, j, 1]
            x_copy(lead, j).start()

            @pl.when(j >= offset)
            def _():
                x_copy(1 - lead, j - offset).start()

        @pl.when(i < n)
        def _():
            local_states(core * n + i, pair.at[core, i])

        return carry

    lax.fori_loop(0, n + 1, first, 0)

    def rest(j, carry):
        @pl.when(j + offset >= n)
        def _():
            x_copy(1 - lead, j).start()

        return carry

    lax.fori_loop(0, n, rest, 0)
    dec_copies[1].wait_recv()
    dec_copies[2].wait_recv()

    @pl.when(jnp.logical_not(has_down))
    def _():
        zrx[0] = jnp.zeros(zrx.shape[1:], F32)

    @pl.when(jnp.logical_not(has_up))
    def _():
        zrx[1] = jnp.zeros(zrx.shape[1:], F32)

    results = (att_out, qg_out, kg_out, vg_out)

    def outputs(head, state, grad):
        cols = lanes(head)
        q, k, v, g = q_ref[:, cols], k_ref[:, cols], v_ref[:, cols], g_ref[:, cols]
        row = cum_ref[pl.ds(head, 1), :]
        col = column(row)
        total = row[:, length - 1 : length]
        causal = col_index <= row_index
        mask = jnp.where(causal, jnp.exp(jnp.where(causal, col - row, 0.0)), 0.0)
        weights = (dot(q, k, 1, 1) * mask).astype(BF16)
        scores = (dot(g, v, 1, 1) * mask).astype(BF16)
        to_query = jnp.exp(col)
        to_end = jnp.exp(total - col)
        state = state.astype(BF16)
        grad = grad.astype(BF16)
        outs[0, :, cols] = (dot(weights, v, 1, 0) + to_query * dot(q, state, 1, 0)).astype(BF16)
        outs[1, :, cols] = (dot(scores, k, 1, 0) + to_query * dot(g, state, 1, 1)).astype(BF16)
        outs[2, :, cols] = (dot(scores, q, 0, 0) + to_end * dot(v, grad, 1, 1)).astype(BF16)
        outs[3, :, cols] = (dot(weights, g, 0, 0) + to_end * dot(k, grad, 1, 0)).astype(BF16)
        for i, dst in enumerate(results):
            pltpu.make_async_copy(outs.at[i, :, cols], dst.at[:, cols], out_sem.at[i]).start()

    lag = HOP_SLOTS * jnp.maximum(z, planes - 1 - z) + 1

    def second(t, carry):
        jf = t - HOP_SLOTS * z

        @pl.when(jnp.logical_and(jf >= 0, jf < n))
        def _():
            head = core * n + jf
            a00, a01 = decay(0, head), decay(1, head)
            a10, a11 = decay(2, head), decay(3, head)
            x_copy(0, jf).wait_recv()

            @pl.when(has_down)
            def _():
                z_copy(0, jf).wait_recv()

            before = zrx[0, jf]
            middle = (a00 * a01) * before + chips[0, 0, jf]

            @pl.when(has_up)
            def _():
                ztx[0, jf] = (a10 * a11) * middle + chips[1, 0, jf]
                z_copy(0, jf).start()

            into = jnp.where(x == 0, before, middle)
            res[0, 0, jf] = into
            res[1, 0, jf] = decay(2 * x, head) * into + pair[0, jf, 0]
            s_copy(0, jf).start()

        jb = t - HOP_SLOTS * (planes - 1 - z)

        @pl.when(jnp.logical_and(jb >= 0, jb < n))
        def _():
            head = core * n + jb
            a00, a01 = decay(0, head), decay(1, head)
            a10, a11 = decay(2, head), decay(3, head)
            x_copy(1, jb).wait_recv()

            @pl.when(has_up)
            def _():
                z_copy(1, jb).wait_recv()

            after = zrx[1, jb]
            middle = (a10 * a11) * after + chips[1, 1, jb]

            @pl.when(has_down)
            def _():
                ztx[1, jb] = (a00 * a01) * middle + chips[0, 1, jb]
                z_copy(1, jb).start()

            into = jnp.where(x == 1, after, middle)
            res[1, 1, jb] = into
            res[0, 1, jb] = decay(2 * x + 1, head) * into + pair[1, jb, 1]
            s_copy(1, jb).start()

        jo = t - lag

        @pl.when(jnp.logical_and(jo >= 0, jo < n))
        def _():
            outputs(core * n + jo, res[core, 0, jo], res[core, 1, jo])
            s_copy(0, jo).wait_recv()
            s_copy(1, jo).wait_recv()
            outputs((1 - core) * n + jo, srx[0, jo], srx[1, jo])

        return carry

    lax.fori_loop(0, n + HOP_SLOTS * (planes - 1) + 1, second, 0)

    for i, dst in enumerate(results):
        pltpu.make_async_copy(outs.at[i], dst, out_sem.at[i]).wait()
    for copy in dec_copies:
        copy.wait_send()

    def drain(j, carry):
        pair_copy(j).wait_send()
        for d in (0, 1):
            x_copy(d, j).wait_send()
            s_copy(d, j).wait_send()

        @pl.when(has_up)
        def _():
            z_copy(0, j).wait_send()

        @pl.when(has_down)
        def _():
            z_copy(1, j).wait_send()

        return carry

    lax.fori_loop(0, n, drain, 0)


def on_device(planes, query_rows, key_rows, value_rows, log_decay, out_grad):
    heads = log_decay.shape[0]
    width = query_rows.shape[1] // heads
    n = heads // 2
    square = (width, width)
    dma = pltpu.SemaphoreType.DMA
    shape = jax.ShapeDtypeStruct(query_rows.shape, BF16)
    return pl.pallas_call(
        functools.partial(kernel, planes),
        out_shape=(shape,) * 4,
        in_specs=[pl.BlockSpec(memory_space=pl.ANY)] * 4
        + [pl.BlockSpec(memory_space=pltpu.VMEM)],
        out_specs=(pl.BlockSpec(memory_space=pl.ANY),) * 4,
        scratch_shapes=[
            pltpu.VMEM((4,) + query_rows.shape, BF16),
            pltpu.VMEM((4,) + query_rows.shape, BF16),
            pltpu.VMEM(log_decay.shape, F32),
            pltpu.VMEM((2, n, 2) + square, F32),
            pltpu.VMEM((n, 2) + square, F32),
            pltpu.VMEM((2, 2, n) + square, F32),
            pltpu.VMEM((2, n) + square, F32),
            pltpu.VMEM((2, n) + square, F32),
            pltpu.VMEM((2, 2, n) + square, F32),
            pltpu.VMEM((2, n) + square, F32),
            pltpu.VMEM((4, heads, width), F32),
            dma((4,)),
            dma((4,)),
            dma((3,)),
            dma((3,)),
            dma((n,)),
            dma((n,)),
            dma((2, n)),
            dma((2, n)),
            dma((2, n)),
            dma((2, n)),
            dma((2, n)),
            dma((2, n)),
        ],
        compiler_params=pltpu.CompilerParams(
            collective_id=0, has_side_effects=True, vmem_limit_bytes=48 * 1024 * 1024
        ),
    )(query_rows, key_rows, value_rows, out_grad, log_decay)


def solution(mesh):
    rows = P(("grp", "seq"), None)
    in_specs = (rows, rows, rows, P(None, ("grp", "seq")), rows)
    return jax.shard_map(
        functools.partial(on_device, mesh.shape["seq"] // 4),
        mesh=mesh,
        in_specs=in_specs,
        out_specs=(rows,) * 4,
        check_vma=False,
    )
```

```python
import functools

import jax
import jax.numpy as jnp
from jax import lax
from jax.experimental import pallas as pl
from jax.experimental.pallas import tpu as pltpu
from jax.sharding import PartitionSpec as P

F32 = jnp.float32
BF16 = jnp.bfloat16
HOP_SLOTS = 5


def dot(a, b, a_dim, b_dim):
    return lax.dot_general(a, b, (((a_dim,), (b_dim,)), ((), ())), preferred_element_type=F32)


def kernel(
    planes,
    q_in,
    k_in,
    v_in,
    g_in,
    log_ref,
    att_out,
    qg_out,
    kg_out,
    vg_out,
    rows,
    outs,
    cum_ref,
    pair,
    give,
    chips,
    ztx,
    zrx,
    res,
    srx,
    dec,
    in_sem,
    out_sem,
    dec_send,
    dec_recv,
    pair_send,
    pair_recv,
    x_send,
    x_recv,
    z_send,
    z_recv,
    s_send,
    s_recv,
):
    n = pair.shape[1]
    width = pair.shape[-1]
    length = rows.shape[1]
    q_ref, k_ref, v_ref, g_ref = (rows.at[i] for i in range(4))
    seq = lax.axis_index("seq")
    core = lax.rem(seq, 2)
    x = lax.rem(seq // 2, 2)
    z = seq // 4
    place = 2 * x + core
    base = 4 * z
    sibling = base + 2 * x + (1 - core)
    across = base + 2 * (1 - x) + core
    diagonal = base + 2 * (1 - x) + (1 - core)
    has_down = z > 0
    has_up = z < planes - 1

    loads = [
        pltpu.make_async_copy(src, rows.at[i], in_sem.at[i])
        for i, src in enumerate((q_in, k_in, v_in, g_in))
    ]
    for load in loads:
        load.start()

    barrier = pltpu.get_barrier_semaphore()
    for peer in (sibling, across, diagonal):
        pl.semaphore_signal(barrier, inc=1, device_id={"seq": peer})

    @pl.when(has_down)
    def _():
        pl.semaphore_signal(barrier, inc=1, device_id={"seq": seq - 4})

    @pl.when(has_up)
    def _():
        pl.semaphore_signal(barrier, inc=1, device_id={"seq": seq + 4})

    row_index = lax.broadcasted_iota(jnp.int32, (length, length), 0)
    col_index = lax.broadcasted_iota(jnp.int32, (length, length), 1)
    cum_ref[...] = lax.dot_general(
        log_ref[...],
        (row_index <= col_index).astype(F32),
        (((1,), (0,)), ((), ())),
        precision=lax.Precision.HIGHEST,
        preferred_element_type=F32,
    )
    dec[place] = jnp.broadcast_to(jnp.exp(cum_ref[:, length - 1 : length]), dec.shape[1:])

    pl.semaphore_wait(barrier, 3 + has_down.astype(jnp.int32) + has_up.astype(jnp.int32))

    def remote(src, dst, send, recv, peer):
        return pltpu.make_async_remote_copy(
            src_ref=src, dst_ref=dst, send_sem=send, recv_sem=recv, device_id={"seq": peer}
        )

    def dec_copy(slot, peer):
        return remote(dec.at[place], dec.at[place], dec_send.at[slot], dec_recv.at[slot], peer)

    def pair_copy(j):
        return remote(give.at[j], pair.at[core, j], pair_send.at[j], pair_recv.at[j], sibling)

    def x_copy(d, j):
        return remote(
            chips.at[x, d, j], chips.at[x, d, j], x_send.at[d, j], x_recv.at[d, j], across
        )

    def z_copy(d, j):
        peer = seq + 4 if d == 0 else seq - 4
        return remote(ztx.at[d, j], zrx.at[d, j], z_send.at[d, j], z_recv.at[d, j], peer)

    def s_copy(d, j):
        return remote(
            res.at[1 - core, d, j], srx.at[d, j], s_send.at[d, j], s_recv.at[d, j], sibling
        )

    dec_copies = [dec_copy(0, sibling), dec_copy(1, across), dec_copy(2, diagonal)]
    for copy in dec_copies:
        copy.start()
    for load in loads:
        load.wait()

    def column(row):
        return jnp.sum(jnp.where(row_index == col_index, row, 0.0), axis=1, keepdims=True)

    def lanes(head):
        return pl.ds(pl.multiple_of(head * width, width), width)

    def decay(p, head):
        return dec[p, pl.ds(head, 1), :]

    def local_states(head, dst):
        cols = lanes(head)
        row = cum_ref[pl.ds(head, 1), :]
        col = column(row)
        total = row[:, length - 1 : length]
        weighted = (k_ref[:, cols].astype(F32) * jnp.exp(total - col)).astype(BF16)
        scaled = (q_ref[:, cols].astype(F32) * jnp.exp(col)).astype(BF16)
        dst[0] = dot(weighted, v_ref[:, cols], 0, 0)
        dst[1] = dot(scaled, g_ref[:, cols], 0, 0)

    lead = jnp.where(2 * z <= planes - 1, 0, 1)
    offset = HOP_SLOTS * jnp.abs(planes - 1 - 2 * z)

    def first(i, carry):
        @pl.when(i < n)
        def _():
            local_states((1 - core) * n + i, give.at[i])
            pair_copy(i).start()

        @pl.when(i == 1)
        def _():
            dec_copies[0].wait_recv()

        @pl.when(i >= 1)
        def _():
            j = i - 1
            head = core * n + j
            pair_copy(j).wait_recv()
            chips[x, 0, j] = decay(2 * x + 1, head) * pair[0, j, 0] + pair[1, j, 0]
            chips[x, 1, j] = decay(2 * x, head) * pair[1, j, 1] + pair[0, j, 1]
            x_copy(lead, j).start()

            @pl.when(j >= offset)
            def _():
                x_copy(1 - lead, j - offset).start()

        @pl.when(i < n)
        def _():
            local_states(core * n + i, pair.at[core, i])

        return carry

    lax.fori_loop(0, n + 1, first, 0)

    def rest(j, carry):
        @pl.when(j + offset >= n)
        def _():
            x_copy(1 - lead, j).start()

        return carry

    lax.fori_loop(0, n, rest, 0)
    dec_copies[1].wait_recv()
    dec_copies[2].wait_recv()

    @pl.when(jnp.logical_not(has_down))
    def _():
        zrx[0] = jnp.zeros(zrx.shape[1:], F32)

    @pl.when(jnp.logical_not(has_up))
    def _():
        zrx[1] = jnp.zeros(zrx.shape[1:], F32)

    results = (att_out, qg_out, kg_out, vg_out)

    def outputs(head, state, grad):
        cols = lanes(head)
        q, k, v, g = q_ref[:, cols], k_ref[:, cols], v_ref[:, cols], g_ref[:, cols]
        row = cum_ref[pl.ds(head, 1), :]
        col = column(row)
        total = row[:, length - 1 : length]
        causal = col_index <= row_index
        mask = jnp.where(causal, jnp.exp(jnp.where(causal, col - row, 0.0)), 0.0)
        weights = (dot(q, k, 1, 1) * mask).astype(BF16)
        scores = (dot(g, v, 1, 1) * mask).astype(BF16)
        to_query = jnp.exp(col)
        to_end = jnp.exp(total - col)
        state = state.astype(BF16)
        grad = grad.astype(BF16)
        outs[0, :, cols] = (dot(weights, v, 1, 0) + to_query * dot(q, state, 1, 0)).astype(BF16)
        outs[1, :, cols] = (dot(scores, k, 1, 0) + to_query * dot(g, state, 1, 1)).astype(BF16)
        outs[2, :, cols] = (dot(scores, q, 0, 0) + to_end * dot(v, grad, 1, 1)).astype(BF16)
        outs[3, :, cols] = (dot(weights, g, 0, 0) + to_end * dot(k, grad, 1, 0)).astype(BF16)
        for i, dst in enumerate(results):
            pltpu.make_async_copy(outs.at[i, :, cols], dst.at[:, cols], out_sem.at[i]).start()

    lag = HOP_SLOTS * jnp.maximum(z, planes - 1 - z) + 1

    def second(t, carry):
        jf = t - HOP_SLOTS * z

        @pl.when(jnp.logical_and(jf >= 0, jf < n))
        def _():
            head = core * n + jf
            a00, a01 = decay(0, head), decay(1, head)
            a10, a11 = decay(2, head), decay(3, head)
            x_copy(0, jf).wait_recv()

            @pl.when(has_down)
            def _():
                z_copy(0, jf).wait_recv()

            before = zrx[0, jf]
            middle = (a00 * a01) * before + chips[0, 0, jf]

            @pl.when(has_up)
            def _():
                ztx[0, jf] = (a10 * a11) * middle + chips[1, 0, jf]
                z_copy(0, jf).start()

            into = jnp.where(x == 0, before, middle)
            res[0, 0, jf] = into
            res[1, 0, jf] = decay(2 * x, head) * into + pair[0, jf, 0]
            s_copy(0, jf).start()

        jb = t - HOP_SLOTS * (planes - 1 - z)

        @pl.when(jnp.logical_and(jb >= 0, jb < n))
        def _():
            head = core * n + jb
            a00, a01 = decay(0, head), decay(1, head)
            a10, a11 = decay(2, head), decay(3, head)
            x_copy(1, jb).wait_recv()

            @pl.when(has_up)
            def _():
                z_copy(1, jb).wait_recv()

            after = zrx[1, jb]
            middle = (a10 * a11) * after + chips[1, 1, jb]

            @pl.when(has_down)
            def _():
                ztx[1, jb] = (a00 * a01) * middle + chips[0, 1, jb]
                z_copy(1, jb).start()

            into = jnp.where(x == 1, after, middle)
            res[1, 1, jb] = into
            res[0, 1, jb] = decay(2 * x + 1, head) * into + pair[1, jb, 1]
            s_copy(1, jb).start()

        jo = t - lag

        @pl.when(jnp.logical_and(jo >= 0, jo < n))
        def _():
            outputs(core * n + jo, res[core, 0, jo], res[core, 1, jo])
            s_copy(0, jo).wait_recv()
            s_copy(1, jo).wait_recv()
            outputs((1 - core) * n + jo, srx[0, jo], srx[1, jo])

        return carry

    lax.fori_loop(0, n + HOP_SLOTS * (planes - 1) + 1, second, 0)

    for i, dst in enumerate(results):
        pltpu.make_async_copy(outs.at[i], dst, out_sem.at[i]).wait()
    for copy in dec_copies:
        copy.wait_send()

    def drain(j, carry):
        pair_copy(j).wait_send()
        for d in (0, 1):
            x_copy(d, j).wait_send()
            s_copy(d, j).wait_send()

        @pl.when(has_up)
        def _():
            z_copy(0, j).wait_send()

        @pl.when(has_down)
        def _():
            z_copy(1, j).wait_send()

        return carry

    lax.fori_loop(0, n, drain, 0)


def on_device(planes, query_rows, key_rows, value_rows, log_decay, out_grad):
    heads = log_decay.shape[0]
    width = query_rows.shape[1] // heads
    n = heads // 2
    square = (width, width)
    dma = pltpu.SemaphoreType.DMA
    shape = jax.ShapeDtypeStruct(query_rows.shape, BF16)
    return pl.pallas_call(
        functools.partial(kernel, planes),
        out_shape=(shape,) * 4,
        in_specs=[pl.BlockSpec(memory_space=pl.ANY)] * 4
        + [pl.BlockSpec(memory_space=pltpu.VMEM)],
        out_specs=(pl.BlockSpec(memory_space=pl.ANY),) * 4,
        scratch_shapes=[
            pltpu.VMEM((4,) + query_rows.shape, BF16),
            pltpu.VMEM((4,) + query_rows.shape, BF16),
            pltpu.VMEM(log_decay.shape, F32),
            pltpu.VMEM((2, n, 2) + square, F32),
            pltpu.VMEM((n, 2) + square, F32),
            pltpu.VMEM((2, 2, n) + square, F32),
            pltpu.VMEM((2, n) + square, F32),
            pltpu.VMEM((2, n) + square, F32),
            pltpu.VMEM((2, 2, n) + square, F32),
            pltpu.VMEM((2, n) + square, F32),
            pltpu.VMEM((4, heads, width), F32),
            dma((4,)),
            dma((4,)),
            dma((3,)),
            dma((3,)),
            dma((n,)),
            dma((n,)),
            dma((2, n)),
            dma((2, n)),
            dma((2, n)),
            dma((2, n)),
            dma((2, n)),
            dma((2, n)),
        ],
        compiler_params=pltpu.CompilerParams(
            collective_id=0, has_side_effects=True, vmem_limit_bytes=48 * 1024 * 1024
        ),
    )(query_rows, key_rows, value_rows, out_grad, log_decay)


def solution(mesh):
    rows = P(("grp", "seq"), None)
    in_specs = (rows, rows, rows, P(None, ("grp", "seq")), rows)
    return jax.shard_map(
        functools.partial(on_device, mesh.shape["seq"] // 4),
        mesh=mesh,
        in_specs=in_specs,
        out_specs=(rows,) * 4,
        check_vma=False,
    )
```
